32 devices in a mesh: mem: 8 (over y, x, core), row: 4 (over z).
Axes of the slice: x: 2, y: 2, z: 4, core: 2. Of those that a mesh axis runs over, the one named last changes fastest.
Arguments:
- decoder_in: bfloat16 [32, 128, 1024], P(('mem', 'row')), may hold values from -6 to 6
- memory: bfloat16 [8, 4, 1024, 1024], P(None, 'row', 'mem'), may hold values from -6 to 6
- cotangent: bfloat16 [32, 128, 1024], P(('mem', 'row')), may hold values from -6 to 6
- dec_lengths: int32 [32], P(('mem', 'row')), may hold values from 32 to 128, as said below
- src_lengths: int32 [8, 4], P(None, 'row'), may hold values from 64 to 1024, as said below
- self_weights: bfloat16 [4, 1024, 1024], P(None, ('mem', 'row'))
- cross_weights: bfloat16 [4, 1024, 1024], P(None, ('mem', 'row'))
- ffn_up: bfloat16 [1024, 4096], P(('mem', 'row')), may hold values from -0.1875 to 0.1875
- ffn_down: bfloat16 [4096, 1024], P(('mem', 'row')), may hold values from -0.09375 to 0.09375
- norm_gains: float32 [3, 1024], replicated, may hold values from 0.25 to 1.75
- prefix: float32 [2, 30, 1024], P(None, None, ('mem', 'row')), may hold values from -6 to 6
- prefix_first: float32 [2, 30, 1024], P(None, None, ('mem', 'row'))
- prefix_second: float32 [2, 30, 1024], P(None, None, ('mem', 'row')), as said below
- down_proj: float32 [1024, 512], P(('mem', 'row')), may hold values from -0.1875 to 0.1875
- down_first: float32 [1024, 512], P(('mem', 'row'))
- down_second: float32 [1024, 512], P(('mem', 'row')), as said below
- up_proj: float32 [512, 1024], P(('mem', 'row')), may hold values from -0.0625 to 0.0625
- up_first: float32 [512, 1024], P(('mem', 'row'))
- up_second: float32 [512, 1024], P(('mem', 'row')), as said below
- biases: float32 [1536], P(('mem', 'row')), may hold values from -4 to 4
- bias_first: float32 [1536], P(('mem', 'row'))
- bias_second: float32 [1536], P(('mem', 'row')), as said below
Outputs:
- block_out: bfloat16 [32, 128, 1024], P(('mem', 'row'))
- decoder_grad: float32 [32, 128, 1024], P(('mem', 'row'))
- memory_grad: float32 [8, 4, 1024, 1024], P(None, 'row', 'mem')
- new_prefix: float32 [2, 30, 1024], P(None, None, ('mem', 'row'))
- new_prefix_first: float32 [2, 30, 1024], P(None, None, ('mem', 'row'))
- new_prefix_second: float32 [2, 30, 1024], P(None, None, ('mem', 'row'))
- new_down: float32 [1024, 512], P(('mem', 'row'))
- new_down_first: float32 [1024, 512], P(('mem', 'row'))
- new_down_second: float32 [1024, 512], P(('mem', 'row'))
- new_up: float32 [512, 1024], P(('mem', 'row'))
- new_up_first: float32 [512, 1024], P(('mem', 'row'))
- new_up_second: float32 [512, 1024], P(('mem', 'row'))
- new_biases: float32 [1536], P(('mem', 'row'))
- new_bias_first: float32 [1536], P(('mem', 'row'))
- new_bias_second: float32 [1536], P(('mem', 'row'))
The draws below stay inside these ranges and needn't reach their ends.
Inputs may be any that keep to these rules, and one draw needn't show every extreme that they name: `dec_lengths`: some sequence has length 128. `src_lengths`: in every column some entry is 1024; the others are at most 400. `prefix_second`: every entry is positive. `down_second`: every entry is positive. `up_second`: every entry is positive. `bias_second`: every entry is positive.
All inputs are finite; a program needn't handle non-finite values.
Results may differ from the reference program's by a relative error of at most 0.035.
Values may be sent and summed in bfloat16 or wider, within the bound.
No kernel may reach another device: no remote copies, remote signals or barrier semaphores. Data moves between devices by JAX's collectives and lax.ppermute only.
A program may use at most 256 MiB of HBM per device.

```python
import jax
import jax.numpy as jnp
from jax import lax

D = 1024
HEADS = 16
HEAD_DIM = 64
FF = 4096
AD = 512
PREFIX = 30
SRC = 1024
LDEC = 128
STEP = 10
NSEQ = 32
N_MEM = 8
N_ROW = 4


def token_root():
    return (NSEQ * LDEC * 0.6) ** 0.5


def first_moment(key, dims_shape, magnitude):
    return (1.0 - 0.9) / 0.9 * magnitude * jax.random.normal(key, dims_shape, jnp.float32)


def second_moment(key, dims_shape, magnitude):
    factor = jnp.exp2(jax.random.uniform(key, dims_shape, jnp.float32, -1.0, 1.0))
    return 2.0 * (1.0 - 0.999) / 0.999 * magnitude * magnitude * factor


def prefix_magnitude():
    return 2.0 * token_root() / (PREFIX + LDEC / 2.0)


def bias_magnitude():
    position = jnp.arange(AD + D)
    return jnp.where(position < AD, 0.7, 3.0) * token_root()


def projection_slabs(key):
    slabs = jnp.sqrt(jnp.array([2.0, 1.0, 1.0, 16.0], jnp.float32) / D)
    return (jax.random.normal(key, (4, D, D), jnp.float32) * slabs[:, None, None]).astype(jnp.bfloat16)


def draw_dec_lengths(key, part):
    key = jax.random.fold_in(key, 11)
    base_key, pick_key = jax.random.split(key)
    drawn = jax.random.randint(base_key, (NSEQ,), LDEC // 4, LDEC + 1)
    chosen = jax.random.randint(pick_key, (), 0, NSEQ)
    return jnp.where(jnp.arange(NSEQ) == chosen, LDEC, drawn).astype(jnp.int32)


def draw_src_lengths(key, part):
    key = jax.random.fold_in(key, 12)
    base_key, pick_key = jax.random.split(key)
    drawn = jax.random.randint(base_key, (N_MEM, N_ROW), SRC // 16, SRC * 25 // 64 + 1)
    chosen = jax.random.randint(pick_key, (N_ROW,), 0, N_MEM)
    return jnp.where(jnp.arange(N_MEM)[:, None] == chosen[None, :], SRC, drawn).astype(jnp.int32)


def draw_self_weights(key, part):
    key = jax.random.fold_in(key, 13)
    return projection_slabs(key)


def draw_cross_weights(key, part):
    key = jax.random.fold_in(key, 14)
    return projection_slabs(key)


def draw_prefix_first(key, part):
    key = jax.random.fold_in(key, 21)
    return first_moment(key, (2, PREFIX, D), prefix_magnitude())


def draw_prefix_second(key, part):
    key = jax.random.fold_in(key, 22)
    return second_moment(key, (2, PREFIX, D), prefix_magnitude())


def draw_down_first(key, part):
    key = jax.random.fold_in(key, 23)
    return first_moment(key, (D, AD), 0.7 * token_root())


def draw_down_second(key, part):
    key = jax.random.fold_in(key, 24)
    return second_moment(key, (D, AD), 0.7 * token_root())


def draw_up_first(key, part):
    key = jax.random.fold_in(key, 25)
    return first_moment(key, (AD, D), 2.0 * token_root())


def draw_up_second(key, part):
    key = jax.random.fold_in(key, 26)
    return second_moment(key, (AD, D), 2.0 * token_root())


def draw_bias_first(key, part):
    key = jax.random.fold_in(key, 27)
    return first_moment(key, (AD + D,), bias_magnitude())


def draw_bias_second(key, part):
    key = jax.random.fold_in(key, 28)
    return second_moment(key, (AD + D,), bias_magnitude())


def steps_of(key, shape, pieces, least, largest):
    gain, own = 1.0, jax.random.fold_in(key, 6)
    for dim, parts in pieces:
        draws = jnp.exp(jax.random.uniform(jax.random.fold_in(own, dim), (parts,), jnp.float32, least / len(pieces), largest / len(pieces)))
        gain = gain * jnp.repeat(draws, shape[dim] // parts).reshape([-1 if axis == dim else 1 for axis in range(len(shape))])
    return gain


def scatter_about(stream_key, shape, deviation, limit, cuts=(), held_as=jnp.bfloat16):
    values = deviation * jax.random.normal(stream_key, shape, jnp.float32)
    if cuts:
        values = values * steps_of(stream_key, shape, cuts, -0.22, 0.18)
    return jnp.clip(values, -limit, limit).astype(held_as)


def setup_inputs(seed: int = 0) -> dict:
    key_list = jax.random.split(jax.random.key(seed), 23)
    return {
        "decoder_in": scatter_about(key_list[0], (NSEQ, LDEC, D), 1.0, 6.0, ((0, 32),)),
        "memory": scatter_about(key_list[1], (N_MEM, N_ROW, SRC, D), 1.0, 6.0, ((1, 4), (2, 8))),
        "cotangent": scatter_about(key_list[2], (NSEQ, LDEC, D), 1.0, 6.0, ((0, 32),)),
        "dec_lengths": draw_dec_lengths(jax.random.fold_in(key_list[22], 71), 0),
        "src_lengths": draw_src_lengths(jax.random.fold_in(key_list[22], 71), 0),
        "self_weights": draw_self_weights(jax.random.fold_in(key_list[22], 71), 0),
        "cross_weights": draw_cross_weights(jax.random.fold_in(key_list[22], 71), 0),
        "ffn_up": scatter_about(key_list[7], (D, FF), D ** -0.5, 0.1875, ((0, 32),)),
        "ffn_down": scatter_about(key_list[8], (FF, D), FF ** -0.5, 0.09375, ((0, 32),)),
        "norm_gains": jnp.clip(1.0 + 0.15 * jax.random.normal(key_list[9], (3, D), jnp.float32), 0.25, 1.75),
        "prefix": scatter_about(key_list[10], (2, PREFIX, D), 1.0, 6.0, ((2, 32),), jnp.float32),
        "prefix_first": draw_prefix_first(jax.random.fold_in(key_list[22], 71), 0),
        "prefix_second": draw_prefix_second(jax.random.fold_in(key_list[22], 71), 0),
        "down_proj": scatter_about(key_list[13], (D, AD), D ** -0.5, 0.1875, ((0, 32),), jnp.float32),
        "down_first": draw_down_first(jax.random.fold_in(key_list[22], 71), 0),
        "down_second": draw_down_second(jax.random.fold_in(key_list[22], 71), 0),
        "up_proj": scatter_about(key_list[16], (AD, D), (16 * AD) ** -0.5, 0.0625, ((0, 32),), jnp.float32),
        "up_first": draw_up_first(jax.random.fold_in(key_list[22], 71), 0),
        "up_second": draw_up_second(jax.random.fold_in(key_list[22], 71), 0),
        "biases": scatter_about(key_list[19], (AD + D,), 0.3, 4.0, ((0, 32),), jnp.float32),
        "bias_first": draw_bias_first(jax.random.fold_in(key_list[22], 71), 0),
        "bias_second": draw_bias_second(jax.random.fold_in(key_list[22], 71), 0),
    }


SCALE = 0.125
NEGATIVE = -1e+30
NORM_EPS = 1e-05
ADAPT_SCALE = 4.0
BETA_ONE = 0.9
BETA_TWO = 0.999
ADAM_EPS = 1e-08
DECAY = 0.01
RATE_PREFIX = 2.0
RATE_DOWN = 0.06
RATE_UP = 0.02
RATE_BIAS = 0.6
HIGHEST = lax.Precision.HIGHEST

@jax.custom_vjp
def low(v):
    return lax.optimization_barrier(v.astype(jnp.bfloat16)).astype(jnp.float32)

@jax.custom_vjp
def low_back(v):
    return v

def low_keep(v):
    return (low(v), None)

def low_pass(kept, grad):
    return (grad,)

def back_keep(v):
    return (v, None)

def back_low(kept, grad):
    return (low(grad),)
low.defvjp(low_keep, low_pass)
low_back.defvjp(back_keep, back_low)

def matmul(left_op, right_op):
    return jnp.matmul(left_op, right_op, precision=HIGHEST)

def layer_norm(hidden, norm_gain):
    center = hidden - lax.optimization_barrier(jnp.mean(hidden, axis=-1, keepdims=True))
    spread = lax.optimization_barrier(jnp.mean(center * center, axis=-1, keepdims=True))
    return center * lax.rsqrt(spread + NORM_EPS) * norm_gain

def attend(queries, keys_all, values_all, allowed):
    batch_size, row_count = (queries.shape[0], queries.shape[1])
    key_count = keys_all.shape[1]
    query_heads = queries.reshape(batch_size, row_count, HEADS, HEAD_DIM)
    key_heads = keys_all.reshape(batch_size, key_count, HEADS, HEAD_DIM)
    value_heads = values_all.reshape(batch_size, key_count, HEADS, HEAD_DIM)
    scores = low_back(SCALE * jnp.einsum('bqhd,bkhd->bhqk', query_heads, key_heads, precision=HIGHEST))
    scores = jnp.where(allowed[:, None], scores, NEGATIVE)
    row_peak = lax.optimization_barrier(jnp.max(scores, axis=-1, keepdims=True))
    exponent = jnp.exp(scores - row_peak)
    probability = exponent / lax.optimization_barrier(jnp.sum(exponent, axis=-1, keepdims=True))
    mixed = jnp.einsum('bhqk,bkhd->bqhd', low(probability), value_heads, precision=HIGHEST)
    return mixed.reshape(batch_size, row_count, HEADS * HEAD_DIM)

def forward(decoder, memory, prefix, down_proj, up_proj, biases, frozen, dec_count, src_count):
    self_weights, cross_weights, ffn_up, ffn_down, norm_gains = frozen
    batch_size, row_count = (decoder.shape[0], decoder.shape[1])
    prefix_low = low(prefix)
    down_low = low(down_proj)
    up_low = low(up_proj)
    bias_low = low(biases)
    queries = low_back(low(matmul(decoder, self_weights[0])))
    keys_tok = low_back(low(matmul(decoder, self_weights[1])))
    values_tok = low_back(low(matmul(decoder, self_weights[2])))
    keys_all = jnp.concatenate([jnp.broadcast_to(prefix_low[0], (batch_size, PREFIX, D)), keys_tok], axis=1)
    values_all = jnp.concatenate([jnp.broadcast_to(prefix_low[1], (batch_size, PREFIX, D)), values_tok], axis=1)
    positions = jnp.arange(row_count)
    causal = (positions[None, :] <= positions[:, None])[None] & (positions[None, None, :] < dec_count[:, None, None])
    allowed = jnp.concatenate([jnp.ones((batch_size, row_count, PREFIX), dtype=bool), causal], axis=2)
    self_mixed = low_back(low(attend(queries, keys_all, values_all, allowed)))
    self_out = low_back(matmul(self_mixed, self_weights[3]))
    first = layer_norm(decoder + self_out, norm_gains[0])
    cross_query = low_back(low(matmul(low(first), cross_weights[0])))
    cross_keys = low_back(low(matmul(memory, cross_weights[1])))
    cross_values = low_back(low(matmul(memory, cross_weights[2])))
    source_ok = (jnp.arange(SRC)[None, :] < src_count[:, None])[:, None, :]
    cross_mixed = low_back(low(attend(cross_query, cross_keys, cross_values, source_ok)))
    cross_out = low_back(matmul(cross_mixed, cross_weights[3]))
    second = layer_norm(first + cross_out, norm_gains[1])
    second_low = low(second)
    hidden = low(jax.nn.gelu(low_back(matmul(second_low, ffn_up)), approximate=False))
    adapt_pre = low_back(matmul(second_low, down_low) + bias_low[:AD])
    adapt_mid = low(jax.nn.gelu(adapt_pre, approximate=False))
    branch = low_back(matmul(hidden, ffn_down) + ADAPT_SCALE * (matmul(adapt_mid, up_low) + bias_low[AD:]))
    return layer_norm(second + branch, norm_gains[2])

def adamw(weight, gradient, moment_one, moment_two, step_rate):
    first = BETA_ONE * moment_one + (1.0 - BETA_ONE) * gradient
    second = BETA_TWO * moment_two + (1.0 - BETA_TWO) * gradient * gradient
    first_hat = first / (1.0 - BETA_ONE ** STEP)
    second_hat = second / (1.0 - BETA_TWO ** STEP)
    updated = weight - step_rate * (first_hat / (jnp.sqrt(second_hat) + ADAM_EPS) + DECAY * weight)
    return (updated, first, second)

def reference(decoder_in, memory, cotangent, dec_lengths, src_lengths, self_weights, cross_weights, ffn_up, ffn_down, norm_gains, prefix, prefix_first, prefix_second, down_proj, down_first, down_second, up_proj, up_first, up_second, biases, bias_first, bias_second):
    frozen = (self_weights.astype(jnp.float32), cross_weights.astype(jnp.float32), ffn_up.astype(jnp.float32), ffn_down.astype(jnp.float32), norm_gains)
    per_group = max(1, min(NSEQ, 4096 // LDEC))
    group_count = NSEQ // per_group
    rows_mask = (jnp.arange(LDEC)[None, :] < dec_lengths[:, None]).astype(jnp.float32)
    weighted = cotangent.astype(jnp.float32) * rows_mask[:, :, None]
    source_len = src_lengths.reshape(NSEQ)
    stacked = (decoder_in.reshape(group_count, per_group, LDEC, D), memory.reshape(group_count, per_group, SRC, D), weighted.reshape(group_count, per_group, LDEC, D), dec_lengths.reshape(group_count, per_group), source_len.reshape(group_count, per_group))

    def one_group(totals, batch_item):
        dec_part, mem_part, cot_part, dec_count, src_count = batch_item

        def run_layer(dec_value, mem_value, pre_value, down_value, up_value, bias_value):
            return forward(dec_value, mem_value, pre_value, down_value, up_value, bias_value, frozen, dec_count, src_count)
        result, pullback = jax.vjp(run_layer, dec_part.astype(jnp.float32), mem_part.astype(jnp.float32), prefix, down_proj, up_proj, biases)
        gradients = pullback(cot_part)
        totals = tuple((running + gradient for running, gradient in zip(totals, gradients[2:])))
        return (totals, (result.astype(jnp.bfloat16), gradients[0], gradients[1]))
    zeros_start = (jnp.zeros_like(prefix), jnp.zeros_like(down_proj), jnp.zeros_like(up_proj), jnp.zeros_like(biases))
    totals, (outputs, dec_grads, mem_grads) = lax.scan(one_group, zeros_start, stacked)
    block_out = outputs.reshape(NSEQ, LDEC, D)
    decoder_grad = dec_grads.reshape(NSEQ, LDEC, D)
    memory_grad = mem_grads.reshape(N_MEM, N_ROW, SRC, D)
    new_prefix = adamw(prefix, totals[0], prefix_first, prefix_second, RATE_PREFIX)
    new_down = adamw(down_proj, totals[1], down_first, down_second, RATE_DOWN)
    new_up = adamw(up_proj, totals[2], up_first, up_second, RATE_UP)
    new_bias = adamw(biases, totals[3], bias_first, bias_second, RATE_BIAS)
    return (block_out, decoder_grad, memory_grad, new_prefix[0], new_prefix[1], new_prefix[2], new_down[0], new_down[1], new_down[2], new_up[0], new_up[1], new_up[2], new_bias[0], new_bias[1], new_bias[2])
```

```python
import functools

import jax
import jax.numpy as jnp
from jax import lax
from jax.experimental import pallas as pl
from jax.experimental.pallas import tpu as pltpu
from jax.sharding import PartitionSpec as P

D = 1024
HEADS = 16
HEAD_DIM = 64
AD = 512
PREFIX = 30
STEP = 10


SCALE = 0.125
NEGATIVE = -1e30
NORM_EPS = 1e-05
ADAPT_SCALE = 4.0
BETA_ONE = 0.9
BETA_TWO = 0.999
ADAM_EPS = 1e-08
DECAY = 0.01
RATE_PREFIX = 2.0
RATE_DOWN = 0.06
RATE_UP = 0.02
RATE_BIAS = 0.6
PAIR = 2 * HEAD_DIM
PAIRS = HEADS // 2
PREFIX_PAD = 32
F32 = jnp.float32
BF16 = jnp.bfloat16
VMEM_LIMIT = 56 * 1024 * 1024
PEAK_PER_MICRO = 1153 * 10**6


def bit_stages(n_mem):
    bits = [1 << b for b in range(1, n_mem.bit_length() - 1)]
    half = len(bits) // 2
    return bits, bits[half:] + bits[:half]


def stage_perm(n_mem, n_row, mem_masks, row_mask=0):
    return [
        (m * n_row + r, (m ^ mem_masks[m & 1]) * n_row + (r ^ row_mask))
        for m in range(n_mem)
        for r in range(n_row)
    ]


def exchange(value, n_mem, n_row, mem_masks, row_mask=0):
    return lax.ppermute(value, ("mem", "row"), stage_perm(n_mem, n_row, mem_masks, row_mask))


def tie(value, *before):
    return lax.optimization_barrier((value,) + before)[0]


def spread_rows(shard, n_mem, n_row):
    row = lax.axis_index("row")
    parts = [shard] + [exchange(shard, n_mem, n_row, (0, 0), dz) for dz in range(1, n_row)]
    slots = []
    for j in range(n_row):
        slot = parts[j]
        for z in range(1, n_row):
            slot = jnp.where(row == z, parts[z ^ j], slot)
        slots.append(slot)
    return jnp.stack(slots)


def spread_rows_at_once(shard, n_row, *before):
    copies = jnp.broadcast_to(shard[None], (n_row,) + shard.shape)
    return lax.all_to_all(tie(copies, *before), "row", 0, 0, tiled=True)


SMALL_ROWS = 16
SMALL_COLS = 32
SMALL_BIAS = 48


def encode_small(prefix, biases):
    n = biases.shape[0] // SMALL_BIAS
    columns_first = prefix.reshape(2, PREFIX, n, SMALL_COLS).transpose(2, 0, 3, 1).reshape(n, -1, PREFIX)
    tiles = jnp.concatenate(
        [
            jnp.pad(columns_first, ((0, 0), (0, 0), (0, 128 - PREFIX))),
            jnp.pad(biases.reshape(n, SMALL_BIAS, 1), ((0, 0), (0, 0), (0, 127))),
        ],
        axis=1,
    ).astype(BF16)
    tiles = tiles.reshape(n, -1, SMALL_ROWS, 128).transpose(0, 2, 1, 3).reshape(n, SMALL_ROWS, -1)
    return jnp.pad(tiles, ((0, 0), (0, 0), (0, D - tiles.shape[2])))


class Lanes:
    def __init__(self):
        self.last, self.count = [None, None], 0

    def send(self, value, n_mem, n_row, masks, which):
        if self.last[which] is not None:
            value = tie(value, self.last[which])
        self.last[which] = exchange(value, n_mem, n_row, masks)
        return self.last[which]


def spread_mem(blocks, lanes, n_mem, n_row, send_gates=(), gates=(), lane=None):
    sends = 0
    for masks in list(zip(*bit_stages(n_mem)))[len(blocks).bit_length() - 1 :]:
        sent = []
        for held in blocks:
            if sends < len(send_gates) and send_gates[sends]:
                held = tie(held, *send_gates[sends])
            sent.append(lanes.send(held, n_mem, n_row, masks, lanes.count % 2 if lane is None else lane))
            lanes.count += 1
            sends += 1
        blocks = blocks + sent
    gates = tuple(gates) + ((),) * (len(blocks) - len(gates))
    return blocks + [
        exchange(tie(held, *gate) if gate else held, n_mem, n_row, (1, 1)) for held, gate in zip(blocks, gates)
    ]


def mem_order(n_mem):
    low, high = bit_stages(n_mem)
    tables = []
    for bits in (low, high):
        table = [0]
        for bit in bits:
            table = table + [entry ^ bit for entry in table]
        tables.append(table)
    own = lax.axis_index("mem")
    zero, one = (jnp.array(table, jnp.int32) for table in tables)
    near = own ^ jnp.where(own % 2 == 0, zero, one)
    far = own ^ 1 ^ jnp.where(own % 2 == 0, one, zero)
    return jnp.concatenate([near, far]).astype(jnp.int32)


def piece_of(blocks, start, rows):
    if rows % 16 == 0:
        return (blocks, start, rows)
    merged = [block[:, start : start + rows].reshape(1, -1, block.shape[-1]) for block in blocks]
    return (merged, 0, merged[0].shape[1])


class Sums:
    def __init__(self, n_mem, n_row):
        self.n_mem, self.n_row = n_mem, n_row
        self.stages = [(bit, bit) for bit in bit_stages(n_mem)[0]] + [(1, 1)]
        self.gone = [[], []]

    def dealt(self):
        own, n_mem = lax.axis_index("mem"), self.n_mem
        lists = []
        for mask in self.stages[0]:
            rest = jnp.array([m for m in range(n_mem) if not m & mask], jnp.int32)
            lists.append(jnp.concatenate([rest + (own & mask), rest + ((own & mask) ^ mask)]))
        return jnp.where(own % 2 == 0, lists[0], lists[1]).astype(jnp.int32)

    def take_all(self, terms):
        self.cube = terms.reshape((2,) * (self.n_mem.bit_length() - 1) + terms.shape[1:])

    def first(self, kept, sent, *after):
        self.cube = kept.reshape((2,) * (self.n_mem.bit_length() - 2) + kept.shape[1:])
        got = exchange(sent, self.n_mem, self.n_row, self.stages[0])
        self.add(self.cube, tie(got, *after).reshape(self.cube.shape))
        self.drop()

    def add(self, one, other):
        self.cube = (one.astype(F32) + other.astype(F32)).astype(BF16)

    def drop(self):
        masks = self.stages.pop(0)
        places = []
        for gone, mask in zip(self.gone, masks):
            axis = self.n_mem.bit_length() - 1 - mask.bit_length()
            places.append(axis - sum(1 for a in gone if a < axis))
            gone.append(axis)
        return masks, places

    def halve(self):
        own = lax.axis_index("mem")
        masks, places = self.drop()

        def take(flip):
            picks = [
                lax.dynamic_index_in_dim(self.cube, ((own & mask) // mask) ^ flip, place, keepdims=False)
                for mask, place in zip(masks, places)
            ]
            return picks[0] if masks[0] == masks[1] else jnp.where(own % 2 == 0, picks[0], picks[1])

        got = exchange(take(1), self.n_mem, self.n_row, masks)
        self.add(take(0), got)

    def cores(self):
        self.stages.insert(0, self.stages.pop())
        self.halve()

    def rows(self, *after):
        row, axis = lax.axis_index("row"), self.cube.ndim - 3
        parts = [lax.dynamic_index_in_dim(self.cube, row ^ dz, axis, keepdims=False) for dz in range(self.n_row)]
        total = parts[0].astype(F32)
        for dz in range(1, self.n_row):
            got = exchange(parts[dz], self.n_mem, self.n_row, (0, 0), dz)
            total = total + (tie(got, *after) if after else got).astype(F32)
        self.cube = total.astype(BF16)


def mm(left_op, right_op):
    return jnp.dot(left_op, right_op, preferred_element_type=F32)


def mm_nt(left_op, right_op):
    return lax.dot_general(left_op, right_op, (((1,), (1,)), ((), ())), preferred_element_type=F32)


def mm_tn(left_op, right_op):
    return lax.dot_general(left_op, right_op, (((0,), (0,)), ((), ())), preferred_element_type=F32)


def norm_forward(hidden):
    center = hidden - jnp.mean(hidden, axis=-1, keepdims=True)
    inverse = lax.rsqrt(jnp.mean(center * center, axis=-1, keepdims=True) + NORM_EPS)
    return center * inverse, inverse


def norm_backward(upstream, norm_gain, normed, inverse):
    scaled = upstream * norm_gain
    return inverse * (
        scaled
        - jnp.mean(scaled, axis=-1, keepdims=True)
        - normed * jnp.mean(scaled * normed, axis=-1, keepdims=True)
    )


def gelu_both(pre_act):
    normal = 0.5 * (1.0 + lax.erf(pre_act * 0.7071067811865476))
    density = 0.3989422804014327 * jnp.exp(-0.5 * pre_act * pre_act)
    return pre_act * normal, normal + pre_act * density


class Loader:
    def __init__(self, order_ref, sems):
        self.order_ref, self.sems, self.used = order_ref, sems, 0

    def start(self, blocks, first, rows, dest):
        copies = []
        for j, block in enumerate(blocks):
            n_row = block.shape[0]
            copies.append(
                pltpu.make_async_copy(
                    block.at[:, pl.ds(first, rows), :],
                    dest.at[pl.ds(self.order_ref[j] * n_row, n_row)],
                    self.sems.at[self.used],
                )
            )
            self.used += 1
        for copy in copies:
            copy.start()
        return copies


def wait_all(copies):
    for copy in copies:
        copy.wait()


def columns(w_ref, cols):
    part = w_ref[:, :, cols]
    return part.reshape(-1, part.shape[-1])


def row_part(w_ref, start, count):
    part = w_ref[pl.ds(start, count)]
    return part.reshape(-1, part.shape[-1])


def tiles_of(total, tile):
    return [pl.ds(t * tile, tile) for t in range(total // tile)]


def stack_heads(pair):
    first = lax.broadcasted_iota(jnp.int32, pair.shape, 1) < HEAD_DIM
    zero = jnp.zeros_like(pair)
    return jnp.concatenate([jnp.where(first, pair, zero), jnp.where(first, zero, pair)], axis=0)


def unstack_heads(both):
    n = both.shape[1] // 2
    own = jnp.concatenate([both[:HEAD_DIM, :n], both[HEAD_DIM:, n:]], axis=0)
    return own.T


def softmax_down(scores):
    peak = jnp.max(scores, axis=0, keepdims=True)
    exponent = jnp.exp(scores - peak)
    return exponent * (1.0 / jnp.sum(exponent, axis=0, keepdims=True))


def self_probability(query_pair, key_pair, dec_len):
    scores = SCALE * mm_nt(key_pair, query_pair)
    key = lax.broadcasted_iota(jnp.int32, scores.shape, 0)
    row_count = query_pair.shape[0] // 2
    query = lax.broadcasted_iota(jnp.int32, scores.shape, 1) % row_count
    seen = ((key <= query) & (key < dec_len)) | ((key >= row_count) & (key < row_count + PREFIX))
    return softmax_down(jnp.where(seen, scores, NEGATIVE))


def self_fwd_kernel(
    firsts, small_first, order, small_order, dec_len, tokens, blocks, small_blocks,
    h_out, q_out, k_out, v_out, bias_out, w, mixed, small, small_sems, sems,
):
    small_loads = Loader(small_order, small_sems).start(small_blocks, small_first, SMALL_ROWS, small)
    loader = Loader(order, sems)
    loads = [loader.start(blocks, first, rows, w.at[i]) for i, (first, rows) in enumerate(firsts)]
    row_count = tokens.shape[0]
    for i, out in enumerate((q_out, k_out, v_out)):
        wait_all(loads[i])
        for cols in tiles_of(D, 512):
            out[pl.ds(0, row_count), cols] = mm(tokens[...], columns(w.at[i], cols)).astype(BF16)
    wait_all(small_loads)

    def across(first, count):
        tiles = [small[:, :, t * 128 : (t + 1) * 128] for t in range(first, first + count)]
        return jnp.concatenate(tiles, axis=1).reshape(-1, 128).astype(F32).T

    each = SMALL_COLS // SMALL_ROWS
    for i, out in enumerate((k_out, v_out)):
        out[pl.ds(row_count, PREFIX_PAD), :] = across(i * each, each)[:PREFIX_PAD].astype(BF16)
    bias_out[...] = across(2 * each, SMALL_BIAS // SMALL_ROWS)[:1]
    for p in range(PAIRS):
        cols = pl.ds(p * PAIR, PAIR)
        probability = self_probability(stack_heads(q_out[:, cols]), k_out[:, cols], dec_len[0])
        both = mm_tn(v_out[:, cols], probability.astype(BF16))
        mixed[:, cols] = unstack_heads(both).astype(BF16)
    wait_all(loads[3])
    for cols in tiles_of(D, 512):
        h_out[:, cols] = tokens[:, cols].astype(F32) + mm(mixed[...], columns(w.at[3], cols))


def cross_kv_kernel(firsts, order, given, blocks, k_out, v_out, memory, w, held, tile_sems, sems):
    loader = Loader(order, sems)
    parts = tiles_of(memory.shape[0], 256)
    wide = tiles_of(D, 256)
    reads = [
        pltpu.make_async_copy(given[0].at[rows], memory.at[rows], tile_sems.at[0, j]) for j, rows in enumerate(parts)
    ]
    for read in reads:
        read.start()
    loads = [loader.start(blocks, first, rows, w.at[i]) for i, (first, rows) in enumerate(firsts)]
    wait_all(reads)
    writes = []
    for i, out in enumerate((k_out, v_out)):
        wait_all(loads[i])
        for t, cols in enumerate(wide):
            weight = columns(w.at[i], cols)
            held[i, :, cols] = mm(memory[...], weight).astype(BF16)
            writes.append(pltpu.make_async_copy(held.at[i, :, cols], out.at[:, cols], tile_sems.at[1 + i, t]))
            writes[-1].start()
    wait_all(writes)


def cross_fwd_kernel(
    firsts, order, src_len, h_one, gains, given, blocks, h_out, q_out, mixed, p_out, w, keys, values, probs, pair_sems, sems
):
    def pair_copies(p):
        cols = pl.ds(p * PAIR, PAIR)
        return [
            pltpu.make_async_copy(given[0].at[:, cols], keys.at[:, cols], pair_sems.at[p, 0]),
            pltpu.make_async_copy(given[1].at[:, cols], values.at[:, cols], pair_sems.at[p, 1]),
        ]

    def write(p):
        return pltpu.make_async_copy(probs.at[p], p_out.at[p], pair_sems.at[p, 2])

    loader = Loader(order, sems)
    loads = [loader.start(blocks, *firsts[0], w.at[0])]
    for p in range(PAIRS):
        for copy in pair_copies(p):
            copy.start()
    loads.append(loader.start(blocks, *firsts[1], w.at[1]))
    normed, unused = norm_forward(h_one[...])
    first = normed * gains[0:1, :]
    wait_all(loads[0])
    low = first.astype(BF16)
    for cols in tiles_of(D, 512):
        q_out[:, cols] = mm(low, columns(w.at[0], cols)).astype(BF16)
    key_count, row_count = keys.shape[0], h_one.shape[0]
    seen = lax.broadcasted_iota(jnp.int32, (key_count, 2 * row_count), 0) < src_len[0]

    def pair(p):
        wait_all(pair_copies(p))
        cols = pl.ds(p * PAIR, PAIR)
        scores = SCALE * mm_nt(keys[:, cols], stack_heads(q_out[:, cols]))
        probability = softmax_down(jnp.where(seen, scores, NEGATIVE)).astype(BF16)
        probs[p] = probability
        write(p).start()
        mixed[:, cols] = unstack_heads(mm_tn(values[:, cols], probability)).astype(BF16)

    for p in range(PAIRS):
        pair(p)

    wait_all(loads[1])
    for cols in tiles_of(D, 512):
        h_out[:, cols] = first[:, cols.start : cols.start + 512] + mm(mixed[...], columns(w.at[1], cols))
    wait_all([write(p) for p in range(PAIRS)])


def ffn_up_kernel(firsts, order, h_two, gains, bias, blocks, hid_out, dhid_out, mid_out, dmid_out, w, sems):
    loader = Loader(order, sems)
    (load,) = [loader.start(blocks, first, rows, w) for first, rows in firsts]
    normed, unused = norm_forward(h_two[...])
    low = (normed * gains[1:2, :]).astype(BF16)
    wait_all(load)
    width = hid_out.shape[1]

    @pl.loop(0, width // 512)
    def tile(t):
        cols = pl.ds(pl.multiple_of(t * 512, 512), 512)
        act, slope = gelu_both(mm(low, columns(w, cols)))
        hid_out[:, cols] = act.astype(BF16)
        dhid_out[:, cols] = slope.astype(BF16)

    act, slope = gelu_both(mm(low, columns(w, pl.ds(width, AD))) + bias[:, :AD])
    mid_out[...] = act.astype(BF16)
    dmid_out[...] = slope.astype(BF16)


def ffn_back_kernel(
    down_firsts, up_firsts, out_firsts, order, dealt, dec_len, h_two, gains, bias, cotangent, hid, dhid, mid, dmid,
    d_blocks, a_blocks, u_blocks, o_blocks,
    block_out, kept, sent, bias_out, g_two_out, g_cross_out, w_down, w_adapt, w_up, w_out, sums, g_pre, held, sems,
):
    loader = Loader(order, sems)
    load_adapt = loader.start(a_blocks, *down_firsts[1], w_adapt)
    load_down = loader.start(d_blocks, *down_firsts[0], w_down)
    load_up = loader.start(u_blocks, *up_firsts[0], w_up)
    load_out = loader.start(o_blocks, *out_firsts[0], w_out)
    row_count, width = hid.shape
    normed_two, inverse_two = norm_forward(h_two[...])
    second = normed_two * gains[1:2, :]
    low = second.astype(BF16)
    wait_all(load_adapt)
    sums[...] = second + ADAPT_SCALE * (mm(mid[...], columns(w_adapt, pl.ds(0, D))) + bias[:, AD:])
    n_row = d_blocks[0].shape[0]
    depth = n_row * w_down.shape[1]
    for j, copy in enumerate(load_down):
        copy.wait()
        place = order[j]
        part = hid[:, pl.ds(pl.multiple_of(place * depth, depth), depth)]
        sums[...] += mm(part, row_part(w_down, place * n_row, n_row))
    normed, inverse = norm_forward(sums[...])
    block_out[...] = (normed * gains[2:3, :]).astype(BF16)
    live = lax.broadcasted_iota(jnp.int32, (row_count, 1), 0) < dec_len[0]
    upstream = cotangent[...].astype(F32) * live.astype(F32)
    g_three = norm_backward(upstream, gains[2:3, :], normed, inverse)
    g_branch = g_three.astype(BF16)
    step = 512 // w_down.shape[1]
    for t in range(width // 512):
        cols = pl.ds(t * 512, 512)
        grad = mm_nt(g_branch, row_part(w_down, t * step, step))
        g_pre[:, cols] = (grad * dhid[:, cols].astype(F32)).astype(BF16)
    grad = ADAPT_SCALE * mm_nt(g_branch, columns(w_adapt, pl.ds(0, D)))
    g_adapt = (grad * dmid[...].astype(F32)).astype(BF16)
    half, n_row = kept.shape[0], kept.shape[1]

    def deal(grad, start):
        size = grad.shape[0]
        share = size // (2 * half)
        held[pl.ds(0, size), :] = grad.astype(BF16)
        rows = pl.ds(start, share // n_row)
        for j in range(half):
            for side, out in enumerate((kept, sent)):
                place = pl.multiple_of(dealt[side * half + j] * share, share)
                out[j, :, rows, :] = held[pl.ds(place, share), :].reshape(n_row, share // n_row, AD)
        return start + share // n_row

    at = deal(mm_tn(low, g_adapt), 0)
    for i in range(D // AD):
        at = deal(ADAPT_SCALE * mm_tn(mid[...], g_branch[:, i * AD : (i + 1) * AD]), at)
    ones = jnp.ones((row_count, 128), BF16)
    bias_out[pl.ds(0, AD), :] = mm_tn(g_adapt, ones).astype(BF16)
    bias_out[pl.ds(AD, D), :] = (ADAPT_SCALE * mm_tn(g_branch, ones)).astype(BF16)
    wait_all(load_up)
    g_two_out[...] = g_three
    step = 512 // w_up.shape[1]
    for t in range(D // 512):
        cols = pl.ds(t * 512, 512)
        part = row_part(w_up, t * step, step)
        g_two_out[:, cols] += mm_nt(g_pre[...], part[:, :width]) + mm_nt(g_adapt, part[:, width:])
    g_two = norm_backward(g_two_out[...], gains[1:2, :], normed_two, inverse_two)
    g_two_out[...] = g_two
    wait_all(load_out)
    low = g_two.astype(BF16)
    step = 512 // w_out.shape[1]
    for t in range(D // 512):
        g_cross_out[:, pl.ds(t * 512, 512)] = mm_nt(low, row_part(w_out, t * step, step)).astype(BF16)


def cross_back_kernel(
    firsts, order, g_cross, queries, mixed, given, blocks,
    dq_out, m_out, w, probs, keys, values, dk, dv, m, pair_sems, tile_sems, sems,
):
    def pair_copies(p):
        cols = pl.ds(p * PAIR, PAIR)
        return [
            pltpu.make_async_copy(given[0].at[p], probs.at[p], pair_sems.at[p, 0]),
            pltpu.make_async_copy(given[1].at[:, cols], keys.at[:, cols], pair_sems.at[p, 1]),
            pltpu.make_async_copy(given[2].at[:, cols], values.at[:, cols], pair_sems.at[p, 2]),
        ]

    for p in range(PAIRS):
        for copy in pair_copies(p):
            copy.start()
    loader = Loader(order, sems)
    loads = [loader.start(blocks, first, rows, w.at[i]) for i, (first, rows) in enumerate(firsts)]

    def pair(p):
        wait_all(pair_copies(p))
        cols = pl.ds(p * PAIR, PAIR)
        up = stack_heads(g_cross[:, cols])
        low = probs[p]
        product = g_cross[:, cols].astype(F32) * mixed[:, cols].astype(F32)
        sums = product.T
        delta = jnp.concatenate(
            [
                jnp.sum(sums[:HEAD_DIM], axis=0, keepdims=True),
                jnp.sum(sums[HEAD_DIM:], axis=0, keepdims=True),
            ],
            axis=1,
        )
        grad_scores = low * (mm_nt(values[:, cols], up) - delta).astype(BF16)
        dq_out[:, cols] = (SCALE * unstack_heads(mm_tn(keys[:, cols], grad_scores))).astype(BF16)
        dk[:, cols] = (SCALE * mm(grad_scores, stack_heads(queries[:, cols]))).astype(BF16)
        dv[:, cols] = mm(low, up).astype(BF16)

    for p in range(PAIRS):
        pair(p)
    for load in loads:
        wait_all(load)
    step = 512 // w.shape[2]

    writes = []
    for t in range(D // 512):
        key_part, value_part = row_part(w.at[0], t * step, step), row_part(w.at[1], t * step, step)
        cols = pl.ds(t * 512, 512)
        m[:, cols] = (mm_nt(dk[...], key_part) + mm_nt(dv[...], value_part)).astype(BF16)
        writes.append(pltpu.make_async_copy(m.at[:, cols], m_out.at[:, cols], tile_sems.at[t]))
        writes[-1].start()
    wait_all(writes)


def self_back_kernel(
    cross_firsts, self_firsts, order, dec_len, g_two, dq_cross, h_one, gains, queries, keys, values, bias_cols,
    c_blocks, s_blocks, d_out, dq, dk, dv, kept, sent, w, g_self, grads, held, sems,
):
    loader = Loader(order, sems)
    load_q = loader.start(c_blocks, *cross_firsts[0], w.at[0])
    load_out = loader.start(s_blocks, *self_firsts[3], w.at[1])
    row_count = g_two.shape[0]
    step = 512 // w.shape[2]
    normed, inverse = norm_forward(h_one[...])
    wait_all(load_q)
    d_out[...] = g_two[...]
    for t in range(D // 512):
        d_out[:, pl.ds(t * 512, 512)] += mm_nt(dq_cross[...], row_part(w.at[0], t * step, step))
    g_one = norm_backward(d_out[...], gains[0:1, :], normed, inverse)
    d_out[...] = g_one
    low = g_one.astype(BF16)
    wait_all(load_out)
    for t in range(D // 512):
        g_self[:, pl.ds(t * 512, 512)] = mm_nt(low, row_part(w.at[1], t * step, step)).astype(BF16)
    for p in range(PAIRS):
        cols = pl.ds(p * PAIR, PAIR)
        stacked = stack_heads(queries[:, cols])
        probability = self_probability(stacked, keys[:, cols], dec_len[0])
        up = stack_heads(g_self[:, cols])
        grad_probs = mm_nt(values[:, cols], up)
        delta = jnp.sum(probability * grad_probs, axis=0, keepdims=True)
        grad_scores = (probability * (grad_probs - delta)).astype(BF16)
        dq[:, cols] = (SCALE * unstack_heads(mm_tn(keys[:, cols], grad_scores))).astype(BF16)
        grad_keys = SCALE * mm(grad_scores, stacked)
        grad_values = mm(probability.astype(BF16), up)
        dk[:, cols] = grad_keys[:row_count].astype(BF16)
        dv[:, cols] = grad_values[:row_count].astype(BF16)
        grads[pl.ds(0, PREFIX_PAD), cols] = grad_keys[row_count:]
        grads[pl.ds(PREFIX_PAD, PREFIX_PAD), cols] = grad_values[row_count:]
    grads[pl.ds(2 * PREFIX_PAD, 128 - 2 * PREFIX_PAD), :] = jnp.zeros((128 - 2 * PREFIX_PAD, D), F32)
    n_mem, n_row, share = held.shape[0], held.shape[1], held.shape[2]
    prefix_share = D // (n_mem * n_row)
    held[:, :, pl.ds(0, prefix_share), :] = grads[...].T.astype(BF16).reshape(n_mem, n_row, prefix_share, 128)
    held[:, :, pl.ds(prefix_share, share - prefix_share), :] = bias_cols[...].reshape(
        n_mem, n_row, share - prefix_share, 128
    )
    core = order[0] % 2
    for chip in range(n_mem // 2):
        kept[chip] = held[2 * chip + core]
        sent[chip] = held[2 * chip + 1 - core]


def token_back_kernel(firsts, order, g_one, dq, dk, dv, blocks, d_out, w, sems):
    loader = Loader(order, sems)
    loads = [loader.start(blocks, *firsts[i], w.at[i]) for i in range(3)]
    step = 512 // w.shape[2]
    for load in loads:
        wait_all(load)
    for t in range(D // 512):
        grad = g_one[:, pl.ds(t * 512, 512)]
        for i, part in enumerate((dq, dk, dv)):
            grad += mm_nt(part[...], row_part(w.at[i], t * step, step))
        d_out[:, pl.ds(t * 512, 512)] = grad


def update_kernel(grads, last, *refs):
    given, outs = refs[:12], refs[12:24]
    across = last[...].T
    width, bias_width = given[0].shape[2], given[9].shape[1]
    down_rows, up_rows = given[3].shape[0], given[6].shape[0]
    up_grad = [
        grads[pl.ds(down_rows + i * up_rows, up_rows), :] for i in range(D // AD)
    ]
    for kind in range(2):
        results = adamw(
            given[0][:, kind, :],
            across[kind * PREFIX_PAD : kind * PREFIX_PAD + PREFIX, :width],
            given[1][:, kind, :],
            given[2][:, kind, :],
            RATE_PREFIX,
        )
        for out, result in zip(outs[:3], results):
            out[:, kind, :] = result
    for at, grad, rate in (
        (3, grads[pl.ds(0, down_rows), :], RATE_DOWN),
        (6, jnp.concatenate(up_grad, axis=1), RATE_UP),
        (9, across[:1, width : width + bias_width], RATE_BIAS),
    ):
        results = adamw(given[at][...], grad, given[at + 1][...], given[at + 2][...], rate)
        for out, result in zip(outs[at : at + 3], results):
            out[...] = result


SMEM = pl.BlockSpec(memory_space=pltpu.SMEM)
VMEM = pl.BlockSpec(memory_space=pltpu.VMEM)
HBM = pl.BlockSpec(memory_space=pltpu.HBM)


def call(kernel, operands, groups, outs, scratch, copies, micros, more=(), far=()):
    count = len(operands)

    def body(*refs):
        given, at = [], count
        for group in groups:
            given.append(refs[at : at + len(group)])
            at += len(group)
        kernel(*refs[:count], *given, *refs[at:])

    blocks = [block for group in groups for block in group]
    return pl.pallas_call(
        body,
        in_specs=[spec for unused, spec in operands] + [HBM] * len(blocks),
        out_specs=[HBM if i in far else VMEM for i in range(len(outs))],
        out_shape=[jax.ShapeDtypeStruct(shape, dtype) for shape, dtype in outs],
        scratch_shapes=[pltpu.VMEM(shape, dtype) for shape, dtype in scratch]
        + [pltpu.SemaphoreType.DMA(shape) for shape in more]
        + [pltpu.SemaphoreType.DMA((copies,))],
        compiler_params=pltpu.CompilerParams(vmem_limit_bytes=VMEM_LIMIT),
        cost_estimate=pl.CostEstimate(flops=micros * PEAK_PER_MICRO, bytes_accessed=0, transcendentals=0),
    )(*[value for value, unused in operands], *blocks)


def group_of(pieces):
    return [list(pieces[0][0])], tuple(piece[1:] for piece in pieces)


def scratch_of(piece, *lead):
    blocks, unused, rows = piece
    return (lead + (len(blocks) * blocks[0].shape[0], rows, blocks[0].shape[-1]), BF16)


def adamw(weight, gradient, moment_one, moment_two, step_rate):
    first = BETA_ONE * moment_one + (1.0 - BETA_ONE) * gradient
    second = BETA_TWO * moment_two + (1.0 - BETA_TWO) * gradient * gradient
    first_hat = first / (1.0 - BETA_ONE**STEP)
    second_hat = second / (1.0 - BETA_TWO**STEP)
    updated = weight - step_rate * (first_hat / (jnp.sqrt(second_hat) + ADAM_EPS) + DECAY * weight)
    return (updated, first, second)


def shards(
    decoder_in,
    memory,
    cotangent,
    dec_lengths,
    src_lengths,
    self_weights,
    cross_weights,
    ffn_up,
    ffn_down,
    norm_gains,
    prefix,
    prefix_first,
    prefix_second,
    down_proj,
    down_first,
    down_second,
    up_proj,
    up_first,
    up_second,
    biases,
    bias_first,
    bias_second,
):
    n_mem, n_row = lax.axis_size("mem"), lax.axis_size("row")
    n_all = n_mem * n_row
    own = lax.axis_index("mem")
    core = own % 2
    prefix_width, bias_width = prefix.shape[2], biases.shape[0]
    self_rows, down_rows, up_rows = self_weights.shape[1], ffn_down.shape[0], up_proj.shape[0]
    ffn_width = ffn_up.shape[1]
    order = mem_order(n_mem)

    up_shard = jnp.concatenate([ffn_up, down_proj.astype(BF16)], axis=1)
    down_shard = jnp.concatenate([ffn_down, up_proj.astype(BF16)], axis=0)
    whole_small = prefix_width % SMALL_COLS == 0 and bias_width % SMALL_BIAS == 0
    if whole_small:
        small = encode_small(prefix, biases).reshape(-1, D)
    else:
        small = jnp.concatenate([prefix.reshape(-1), biases]).astype(BF16)
        small = jnp.pad(small, (0, SMALL_ROWS * D - small.shape[0])).reshape(SMALL_ROWS, D)
    self_shard = jnp.concatenate([self_weights.reshape(-1, D), small], axis=0)

    lanes = Lanes()
    memory_seq = lax.all_to_all(memory[:, 0], "mem", 0, 0, tiled=True).reshape(-1, D)
    cross_held = spread_rows(cross_weights.reshape(-1, D), n_mem, n_row)
    cross_all = spread_mem([cross_held], lanes, n_mem, n_row)
    self_held = spread_rows_at_once(self_shard, n_row, cross_held, memory_seq)
    down_near = exchange(down_shard, n_mem, n_row, next(zip(*bit_stages(n_mem))))
    up_held = spread_rows_at_once(up_shard, n_row, self_held, down_near)

    tokens = decoder_in[0]
    rows = tokens.shape[0]
    keys_self = rows + PREFIX_PAD
    source = memory_seq.shape[0]
    source_len = lax.dynamic_index_in_dim(src_lengths[:, 0], own, 0)

    cross_pieces = [piece_of(cross_all, i * self_rows, self_rows) for i in range(4)]
    refs, firsts = group_of(cross_pieces[1:3])
    k_cross, v_cross = call(
        functools.partial(cross_kv_kernel, firsts),
        [(order, SMEM)],
        [[memory_seq]] + refs,
        [((source, D), BF16), ((source, D), BF16)],
        [((source, D), BF16), scratch_of(cross_pieces[1], 2), ((2, source, D), BF16)],
        2 * n_mem,
        4,
        [(3, max(source, D) // 256)],
        (0, 1),
    )
    self_all = spread_mem([self_held], lanes, n_mem, n_row)
    self_pieces = [piece_of(self_all, i * self_rows, self_rows) for i in range(4)]
    small_first = 4 * self_rows
    if whole_small:
        small_blocks, small_order = list(self_all), order
    else:
        tails = jnp.stack([block[:, small_first : small_first + SMALL_ROWS].reshape(n_row, -1) for block in self_all])
        tails = jnp.zeros_like(tails).at[order].set(tails).reshape(n_all, -1)
        prefix_all = tails[:, : prefix.size].reshape(n_all, 2, PREFIX, -1).transpose(1, 2, 0, 3).reshape(2, PREFIX, D)
        biases_all = tails[:, prefix.size : prefix.size + bias_width].reshape(-1)
        small_blocks, small_order = [encode_small(prefix_all, biases_all)], jnp.zeros((1,), jnp.int32)
        small_first = 0
    down_held = spread_rows_at_once(down_shard, n_row, up_held)
    down_near_held = spread_rows_at_once(down_near, n_row, down_held)
    refs, firsts = group_of(self_pieces)
    h_one, q_self, k_self, v_self, bias_row = call(
        functools.partial(self_fwd_kernel, firsts, small_first),
        [(order, SMEM), (small_order, SMEM), (dec_lengths, SMEM), (tokens, VMEM)],
        refs + [small_blocks],
        [((rows, D), F32), ((rows, D), BF16), ((keys_self, D), BF16), ((keys_self, D), BF16), ((1, AD + D), F32)],
        [scratch_of(self_pieces[0], 4), ((rows, D), BF16), ((D // SMALL_COLS, SMALL_ROWS, D), BF16)],
        4 * n_mem,
        3,
        [(len(small_blocks),)],
    )
    refs, firsts = group_of([cross_pieces[0], cross_pieces[3]])
    h_two, q_cross, mixed_cross, probs = call(
        functools.partial(cross_fwd_kernel, firsts),
        [(order, SMEM), (source_len, SMEM), (h_one, VMEM), (norm_gains, VMEM)],
        [[k_cross, v_cross]] + refs,
        [((rows, D), F32), ((rows, D), BF16), ((rows, D), BF16), ((PAIRS, source, 2 * rows), BF16)],
        [scratch_of(cross_pieces[0], 2)]
        + [((source, D), BF16), ((source, D), BF16), ((PAIRS, source, 2 * rows), BF16)],
        2 * n_mem,
        4,
        [(PAIRS, 3)],
        (3,),
    )
    up_all = spread_mem([up_held], lanes, n_mem, n_row, ((), (k_cross,), (h_one,)), ((), (), (), (h_two,)))
    up_piece = piece_of(up_all, 0, ffn_up.shape[0])
    refs, firsts = group_of([up_piece])
    hid, dhid, mid, dmid = call(
        functools.partial(ffn_up_kernel, firsts),
        [(order, SMEM), (h_two, VMEM), (norm_gains, VMEM), (bias_row, VMEM)],
        refs,
        [((rows, ffn_width), BF16), ((rows, ffn_width), BF16), ((rows, AD), BF16), ((rows, AD), BF16)],
        [scratch_of(up_piece)],
        n_mem,
        3,
    )
    down_all = spread_mem([down_held, down_near_held], lanes, n_mem, n_row, ((), (h_two,)), ((), (), (hid,)), 1)
    down_piece = piece_of(down_all, 0, down_rows)
    adapt_piece = piece_of(down_all, down_rows, up_rows)
    down_refs, down_firsts = group_of([down_piece])
    adapt_refs, adapt_firsts = group_of([adapt_piece])
    up_refs, up_firsts = group_of([up_piece])
    out_refs, out_firsts = group_of([cross_pieces[3]])
    sums = Sums(n_mem, n_row)
    packed_rows = (D + AD * D // AD) // n_all
    block_out, kept, sent, grad_bias, g_two, g_cross = call(
        functools.partial(ffn_back_kernel, down_firsts + adapt_firsts, up_firsts, out_firsts),
        [(order, SMEM), (sums.dealt(), SMEM), (dec_lengths, SMEM), (h_two, VMEM), (norm_gains, VMEM)]
        + [(bias_row, VMEM), (cotangent[0], VMEM)]
        + [(hid, VMEM), (dhid, VMEM), (mid, VMEM), (dmid, VMEM)],
        down_refs + adapt_refs + up_refs + out_refs,
        [((rows, D), BF16), ((n_mem // 2, n_row, packed_rows, AD), BF16), ((n_mem // 2, n_row, packed_rows, AD), BF16), ((AD + D, 128), BF16), ((rows, D), F32), ((rows, D), BF16)],
        [scratch_of(down_piece), scratch_of(adapt_piece), scratch_of(up_piece), scratch_of(cross_pieces[3])]
        + [((rows, D), F32), ((rows, ffn_width), BF16), ((D, AD), BF16)],
        4 * n_mem,
        1,
    )
    refs, firsts = group_of(cross_pieces[1:3])
    dq_cross, memory_seq_grad = call(
        functools.partial(cross_back_kernel, firsts),
        [(order, SMEM), (g_cross, VMEM), (q_cross, VMEM), (mixed_cross, VMEM)],
        [[probs, k_cross, v_cross]] + refs,
        [((rows, D), BF16), ((source, D), BF16)],
        [scratch_of(cross_pieces[1], 2), (probs.shape, BF16)] + [((source, D), BF16)] * 5,
        2 * n_mem,
        1,
        [(PAIRS, 3), (D // 512,)],
        (1,),
    )
    memory_grad = lax.all_to_all(memory_seq_grad.reshape(n_mem, -1, D), "mem", 0, 0, tiled=True)
    cross_refs, cross_firsts = group_of(cross_pieces[:1])
    refs, firsts = group_of(self_pieces)
    share = prefix_width + bias_width
    dealt_shape = (n_mem // 2, n_row, share, 128)
    g_one, dq, dk, dv, last_kept, last_sent = call(
        functools.partial(self_back_kernel, cross_firsts, firsts),
        [(order, SMEM), (dec_lengths, SMEM), (g_two, VMEM), (dq_cross, VMEM), (h_one, VMEM), (norm_gains, VMEM)]
        + [(q_self, VMEM), (k_self, VMEM), (v_self, VMEM), (grad_bias, VMEM)],
        cross_refs + refs,
        [((rows, D), F32)] + [((rows, D), BF16)] * 3 + [(dealt_shape, BF16)] * 2,
        [scratch_of(self_pieces[0], 2), ((rows, D), BF16), ((128, D), F32), ((n_mem, n_row, share, 128), BF16)],
        2 * n_mem,
        1,
    )
    sums.first(kept, sent, g_one)
    last = Sums(n_mem, n_row)
    last.stages = last.stages[-1:] + last.stages[:-1]
    last.first(last_kept, last_sent, g_one)
    sums.cores()
    (decoder_grad,) = call(
        functools.partial(token_back_kernel, firsts),
        [(order, SMEM), (tie(g_one, sums.cube, last.cube), VMEM), (dq, VMEM), (dk, VMEM), (dv, VMEM)],
        refs,
        [((rows, D), F32)],
        [scratch_of(self_pieces[0], 3)],
        3 * n_mem,
        1,
    )
    last.rows()
    sums.rows(decoder_grad)
    last.cube = tie(last.cube, memory_grad)
    last.halve()
    flat = last.cube.reshape(last.cube.shape[:-2] + (-1,))
    last_width = flat.shape[-1]
    last_rows = pl.cdiv(last_width, 16 * AD) * 16
    flat = jnp.pad(flat, ((0, 0),) * (flat.ndim - 1) + ((0, last_rows * AD - last_width),))
    sums.cube = jnp.concatenate([sums.cube, flat.reshape(flat.shape[:-1] + (last_rows, AD))], axis=-2)
    while sums.stages:
        sums.halve()
    reduced = sums.cube.astype(F32)
    own_last = reduced[packed_rows:].reshape(-1, 128)
    if own_last.shape[0] < 128:
        own_last = jnp.pad(own_last, ((0, 128 - own_last.shape[0]), (0, 0)))
    own_last = own_last[:128]
    flat_bias = (1, bias_width)
    states = [value.transpose(1, 0, 2) for value in (prefix, prefix_first, prefix_second)]
    states += [down_proj, down_first, down_second, up_proj, up_first, up_second]
    states += [value.reshape(flat_bias) for value in (biases, bias_first, bias_second)]
    updated = call(
        update_kernel,
        [(reduced, VMEM), (own_last, VMEM)] + [(value, VMEM) for value in states],
        [],
        [(value.shape, F32) for value in states],
        [],
        1,
        1,
    )
    return (
        block_out[None],
        decoder_grad[None],
        memory_grad.astype(F32)[:, None],
        *[value.transpose(1, 0, 2) for value in updated[:3]],
        *updated[3:9],
        *[value.reshape(bias_width) for value in updated[9:]],
    )


def solution(mesh):
    in_specs = (
        P(("mem", "row"), None, None),
        P(None, "row", "mem", None),
        P(("mem", "row"), None, None),
        P(("mem", "row")),
        P(None, "row"),
        P(None, ("mem", "row"), None),
        P(None, ("mem", "row"), None),
        P(("mem", "row"), None),
        P(("mem", "row"), None),
        P(),
        P(None, None, ("mem", "row")),
        P(None, None, ("mem", "row")),
        P(None, None, ("mem", "row")),
        P(("mem", "row"), None),
        P(("mem", "row"), None),
        P(("mem", "row"), None),
        P(("mem", "row"), None),
        P(("mem", "row"), None),
        P(("mem", "row"), None),
        P(("mem", "row")),
        P(("mem", "row")),
        P(("mem", "row")),
    )
    out_specs = (
        P(("mem", "row"), None, None),
        P(("mem", "row"), None, None),
        P(None, "row", "mem", None),
        P(None, None, ("mem", "row")),
        P(None, None, ("mem", "row")),
        P(None, None, ("mem", "row")),
        P(("mem", "row"), None),
        P(("mem", "row"), None),
        P(("mem", "row"), None),
        P(("mem", "row"), None),
        P(("mem", "row"), None),
        P(("mem", "row"), None),
        P(("mem", "row")),
        P(("mem", "row")),
        P(("mem", "row")),
    )
    return jax.shard_map(shards, mesh=mesh, in_specs=in_specs, out_specs=out_specs, check_vma=False)
```
